256 devices in a mesh: row: 8 (over z), col: 16 (over y, x_lo, core), rep: 2 (over x_hi).
Axes of the slice: x: 4 (x_hi: 2, x_lo: 2; x = x_hi * 2 + x_lo), y: 4, z: 8, core: 2. Of those that a mesh axis runs over, the one named last changes fastest.
Arguments:
- hamiltonian: bfloat16 [8192, 8192], P('row', ('rep', 'col')), may hold values from -0.109375 to 0.109375
- density: bfloat16 [8192, 8192], P(('rep', 'row'), 'col'), may hold values from -6 to 6
- ham_pattern: int32 [128, 128], P('row', ('rep', 'col')), may hold values 0 or 1
- den_pattern: int32 [128, 128], P(('rep', 'row'), 'col'), may hold values 0 or 1
- tile_basis: bfloat16 [64, 16, 2048], P(None, None, 'col'), may hold values from -0.75 to 0.75
- offsets: int32 [128], P(('row', 'rep')), may hold values from 0 to 31
Outputs:
- product: bfloat16 [8192, 8192], P(('row', 'rep'), 'col')
- grid_density: float32 [512, 2048], P(('row', 'rep'), 'col')
The draws below stay inside these ranges and needn't reach their ends.
All inputs are finite; a program needn't handle non-finite values. No bound on the sum of `ham_pattern` or of `den_pattern` on one device may be relied on, other than what follows from the above.
Results may differ from the reference program's by a relative error of at most 0.0004.
Values may be sent and summed in bfloat16 or wider, within the bound.
No kernel may reach another device: no remote copies, remote signals or barrier semaphores. Data moves between devices by JAX's collectives and lax.ppermute only.
A program may use at most 128 MiB of HBM per device.

```python
import math
import jax
import jax.numpy as jnp
from jax import lax

BLK = 64
SX = 32
TX = 16
NB = 128
ATOMS_DEV = 8
NXG = 512
PL = 2048


def with_ends(array, rng, smallest, high):
    longest = array.shape.index(max(array.shape))
    spots = []
    for shift in (0, 1):
        where = [jax.random.randint(jax.random.fold_in(rng, axis), (), 0, length) for axis, length in enumerate(array.shape)]
        where[longest] = (where[longest] + shift) % array.shape[longest]
        spots.append(tuple(where))
    return array.at[spots[0]].set(smallest).at[spots[1]].set(high)


def level_of(stream_key, extent, shards, smallest, largest):
    loudness, own = 1.0, jax.random.fold_in(stream_key, 6)
    for dim, blocks in shards:
        draws = jnp.exp(jax.random.uniform(jax.random.fold_in(own, dim), (blocks,), jnp.float32, smallest / len(shards), largest / len(shards)))
        loudness = loudness * jnp.repeat(draws, extent[dim] // blocks).reshape([-1 if axis == dim else 1 for axis in range(len(extent))])
    return loudness


def centred(own_key, shape, scale, limit, pieces=(), kind=jnp.bfloat16):
    drawn = scale * jax.random.normal(own_key, shape, jnp.float32)
    if pieces:
        drawn = drawn * level_of(own_key, shape, pieces, -0.22, 0.18)
    return jnp.clip(drawn, -limit, limit).astype(kind)


def setup_inputs(seed: int = 0) -> dict:
    key_list = jax.random.split(jax.random.key(seed), 7)
    return {
        "hamiltonian": centred(key_list[0], (NB * BLK, NB * BLK), (NB * BLK // 3) ** -0.5, 0.109375, ((0, 8), (1, 32))),
        "density": centred(key_list[1], (NB * BLK, NB * BLK), 1.0, 6.0, ((0, 16), (1, 16))),
        "ham_pattern": with_ends((jax.random.randint(key_list[2], (NB, NB), 0, 3) < 1).astype(jnp.int32), jax.random.fold_in(key_list[2], 1), 0, 1),
        "den_pattern": with_ends((jax.random.randint(key_list[3], (NB, NB), 0, 3) < 1).astype(jnp.int32), jax.random.fold_in(key_list[3], 1), 0, 1),
        "tile_basis": centred(key_list[4], (BLK, TX, PL), BLK ** -0.5, 0.75, ((2, 16),)),
        "offsets": with_ends(jax.random.randint(key_list[5], (NB,), 0, SX), jax.random.fold_in(key_list[5], 1), 0, SX - 1).astype(jnp.int32),
    }


def expand(matrix, pattern):
    rows_b, cols_b = pattern.shape
    weight = pattern.astype(matrix.dtype)
    shaped = matrix.reshape(rows_b, BLK, cols_b, BLK) * weight[:, None, :, None]
    return shaped.reshape(matrix.shape)

def reference(hamiltonian, density, ham_pattern, den_pattern, tile_basis, offsets):
    ham = expand(hamiltonian, ham_pattern)
    dens = expand(density, den_pattern)
    full = jnp.dot(ham, dens, preferred_element_type=jnp.float32)
    charges = lax.optimization_barrier(jnp.sum(full, axis=1)) * (1.0 / math.sqrt(NB * BLK))
    amplitudes = charges.reshape(NB, BLK)
    tiles = jnp.einsum('am,mtp->atp', amplitudes, tile_basis.astype(jnp.float32), precision=lax.Precision.HIGHEST)
    slab = jnp.arange(NB, dtype=jnp.int32) // ATOMS_DEV
    first = slab * SX + offsets.astype(jnp.int32)
    planes = (first[:, None] + jnp.arange(TX, dtype=jnp.int32)[None, :]) % NXG
    onehot = (planes[:, :, None] == jnp.arange(NXG, dtype=jnp.int32)[None, None, :]).astype(jnp.float32)
    grid_density = jnp.einsum('atx,atp->xp', onehot, tiles, precision=lax.Precision.HIGHEST)
    return (full.astype(jnp.bfloat16), grid_density)
```

```python
import functools
import math

import jax
import jax.numpy as jnp
from jax import lax
from jax.experimental import pallas as pl
from jax.experimental.pallas import tpu as pltpu
from jax.sharding import PartitionSpec as P

SX = 32
TX = 16
BLK = 64
MIB = 1 << 20

NZ = 8
NY = 4
CHUNKS = 2
F32 = jnp.float32
BF16 = jnp.bfloat16


def over_row(value, steps):
    return lax.ppermute(value, "row", [(i, (i + steps) % NZ) for i in range(NZ)])


def row_swap(value, bit):
    return lax.ppermute(value, "row", [(i, i ^ bit) for i in range(NZ)])


def over_y(value, steps):
    pairs = []
    for c in range(4 * NY):
        pairs.append((c, ((c // 4 + steps) % NY) * 4 + c % 4))
    return lax.ppermute(value, "col", pairs)


def col_swap(value, bit):
    return lax.ppermute(value, "col", [(c, c ^ bit) for c in range(4 * NY)])


def rep_swap(value):
    return lax.ppermute(value, "rep", [(0, 1), (1, 0)])


def spread(pattern_ref, rows, cols):
    pattern = pattern_ref[...].astype(F32).astype(BF16)
    rows_b, cols_b = pattern.shape
    left = (
        lax.broadcasted_iota(jnp.int32, (rows, rows_b), 0) // BLK
        == lax.broadcasted_iota(jnp.int32, (rows, rows_b), 1)
    )
    right = (
        lax.broadcasted_iota(jnp.int32, (cols_b, cols), 1) // BLK
        == lax.broadcasted_iota(jnp.int32, (cols_b, cols), 0)
    )
    wide = jnp.dot(pattern, right.astype(F32).astype(BF16), preferred_element_type=F32)
    return jnp.dot(
        left.astype(F32).astype(BF16), wide.astype(BF16), preferred_element_type=F32
    ).astype(BF16)


def dens_mask_kernel(pattern_ref, dens_ref, *chunk_refs):
    rows, cols = dens_ref.shape
    masked = dens_ref[...] * spread(pattern_ref, rows, cols)
    width = cols // len(chunk_refs)
    for i, ref in enumerate(chunk_refs):
        ref[...] = masked[:, i * width : (i + 1) * width]


def ham_mask_kernel(pattern_ref, ham_ref, out_ref):
    rows, cols = ham_ref.shape
    out_ref[...] = ham_ref[...] * spread(pattern_ref, rows, cols)


def mask_dens(pattern, dens):
    rows, cols = dens.shape
    shapes = [jax.ShapeDtypeStruct((rows, cols // CHUNKS), BF16)] * CHUNKS
    return pl.pallas_call(
        dens_mask_kernel,
        out_shape=shapes,
        compiler_params=pltpu.CompilerParams(vmem_limit_bytes=24 * MIB),
        name="mask_dens",
    )(pattern, dens)


def mask_ham(pattern, ham):
    return pl.pallas_call(
        ham_mask_kernel,
        out_shape=jax.ShapeDtypeStruct(ham.shape, BF16),
        compiler_params=pltpu.CompilerParams(vmem_limit_bytes=24 * MIB),
        name="mask_ham",
    )(pattern, ham)


def place():
    row = lax.axis_index("row")
    col = lax.axis_index("col")
    return row, col // 4, (col // 2) % 2, col % 2, lax.axis_index("rep")


def rows_kernel(other, *refs):
    n_ham, n_den = len(HAM_KEYS), NZ * CHUNKS
    ham_refs, den_refs = refs[:n_ham], refs[n_ham : n_ham + n_den]
    out_ref, sums_ref, ham_buf = refs[n_ham + n_den :]
    row, y, x, core, rep = place()
    part = (1 - rep) if other else rep
    rows = out_ref.shape[0]
    first = pl.multiple_of(part * rows, rows)
    for n, (dy, dx, dk) in enumerate(HAM_KEYS):
        chip = lax.rem(y + dy, NY) * 2 + (x + dx - 2 * x * dx)
        half = core + dk - 2 * core * dk
        ham_buf[chip, half] = ham_refs[n][pl.ds(first, rows), :]
    half = ham_buf.shape[3]
    width = out_ref.shape[1] // CHUNKS
    for s in range(NZ):
        chip = lax.rem(row + s, NZ)
        for i in range(CHUNKS):
            den_ref = den_refs[s * CHUNKS + i]
            term = jnp.dot(ham_buf[chip, 0], den_ref[:half], preferred_element_type=F32)
            term += jnp.dot(ham_buf[chip, 1], den_ref[half:], preferred_element_type=F32)
            cols = pl.ds(i * width, width)
            if s == 0:
                out_ref[:, cols] = term
            else:
                out_ref[:, cols] += term
    lanes = 128
    folded = out_ref[:, :lanes]
    for j in range(lanes, out_ref.shape[1], lanes):
        folded += out_ref[:, j : j + lanes]
    sums_ref[...] = lax.dot_general(
        jnp.ones((8, lanes), F32),
        folded,
        (((1,), (1,)), ((), ())),
        precision=lax.Precision.HIGHEST,
        preferred_element_type=F32,
    )


def rows_of(other, ham_blocks, den_blocks):
    rows = ham_blocks[0].shape[0] // 2
    half = ham_blocks[0].shape[1]
    depth = den_blocks[0].shape[0]
    cols = den_blocks[0].shape[1] * CHUNKS
    n = len(ham_blocks) + len(den_blocks)
    return pl.pallas_call(
        functools.partial(rows_kernel, other),
        out_shape=(
            jax.ShapeDtypeStruct((rows, cols), F32),
            jax.ShapeDtypeStruct((8, rows), F32),
        ),
        in_specs=[pl.BlockSpec(memory_space=pltpu.VMEM)] * n,
        scratch_shapes=[pltpu.VMEM((NZ, 2, rows, half), BF16)],
        compiler_params=pltpu.CompilerParams(vmem_limit_bytes=30 * MIB),
        cost_estimate=pl.CostEstimate(
            flops=2 * rows * cols * depth * NZ, bytes_accessed=8 * MIB, transcendentals=0
        ),
        name="rows_other" if other else "rows_own",
    )(*ham_blocks, *den_blocks)


HAM_KEYS = [(dy, dx, dk) for dy in range(NY) for dx in range(2) for dk in range(2)]


def gather_dens(chunks):
    den = [[None] * CHUNKS for _ in range(NZ)]
    den[0] = list(chunks)
    up, down = list(chunks), list(chunks)
    for step in range(1, 5):
        for i in range(CHUNKS):
            if step < 4 or i % 2 == 0:
                up[i] = over_row(up[i], 1)
                den[(NZ - step) % NZ][i] = up[i]
        for i in range(CHUNKS):
            if step < 4 or i % 2 == 1:
                down[i] = over_row(down[i], -1)
                den[step][i] = down[i]
    return [block for blocks in den for block in blocks]


def gather_ham(ham):
    got = {(0, 0): ham}
    got[(3, 0)] = over_y(ham, 1)
    got[(1, 0)] = over_y(ham, -1)
    got[(0, 1)] = col_swap(ham, 2)
    got[(3, 1)] = over_y(got[(0, 1)], 1)
    got[(1, 1)] = over_y(got[(0, 1)], -1)
    got[(2, 0)] = over_y(got[(3, 0)], 1)
    got[(2, 1)] = over_y(got[(1, 1)], -1)
    blocks = {}
    for (dy, dx), block in got.items():
        blocks[(dy, dx, 0)] = block
        blocks[(dy, dx, 1)] = col_swap(block, 1)
    return [blocks[key] for key in HAM_KEYS]


def shards(hamiltonian, density, ham_pattern, den_pattern, tile_basis, offsets):
    chunks = mask_dens(den_pattern, density)
    ham = mask_ham(ham_pattern, hamiltonian)
    den_blocks = gather_dens(chunks)
    ham_blocks = gather_ham(ham)

    part, part_sums = rows_of(True, ham_blocks, den_blocks)
    sent = rep_swap(part)
    part_sums = rep_swap(part_sums)
    kept, sums = rows_of(False, ham_blocks, den_blocks)
    product = (kept + sent).astype(BF16)

    sums = sums + part_sums
    for bit in (1, 2, 4, 8):
        sums = sums + col_swap(sums, bit)
    charges = sums[:1]
    total_order = density.shape[1] * lax.axis_size("col")
    atoms = offsets.shape[0]
    amplitudes = (charges * (1.0 / math.sqrt(total_order))).reshape(atoms, -1)
    tiles = jnp.einsum(
        "am,mtp->atp", amplitudes, tile_basis.astype(F32), precision=lax.Precision.HIGHEST
    )
    planes = offsets[:, None] + jnp.arange(TX, dtype=jnp.int32)[None, :]
    onehot = (planes[:, :, None] == jnp.arange(SX + TX, dtype=jnp.int32)[None, None, :]).astype(F32)
    extended = jnp.einsum("atx,atp->xp", onehot, tiles, precision=lax.Precision.HIGHEST)
    own_planes = extended[:SX]
    count = lax.axis_size("row") * lax.axis_size("rep")
    incoming = lax.ppermute(
        extended[SX:], ("row", "rep"), [(i, (i + 1) % count) for i in range(count)]
    )
    grid_density = jnp.concatenate([own_planes[:TX] + incoming, own_planes[TX:]], axis=0)

    return (product, grid_density)


def solution(mesh):
    in_specs = (
        P("row", ("rep", "col")),
        P(("rep", "row"), "col"),
        P("row", ("rep", "col")),
        P(("rep", "row"), "col"),
        P(None, None, "col"),
        P(("row", "rep")),
    )
    out_specs = (P(("row", "rep"), "col"), P(("row", "rep"), "col"))
    return jax.shard_map(shards, mesh=mesh, in_specs=in_specs, out_specs=out_specs, check_vma=False)
```

```python
import functools
import math

import jax
import jax.numpy as jnp
from jax import lax
from jax.experimental import pallas as pl
from jax.experimental.pallas import tpu as pltpu
from jax.sharding import PartitionSpec as P

SX = 32
TX = 16
BLK = 64
MIB = 1 << 20

NZ = 8
NY = 4
F32 = jnp.float32
BF16 = jnp.bfloat16
FIRST = 256


def way(core):
    return 1 - 2 * core


def over_row(value, steps):
    pairs = []
    for r in range(NZ):
        for c in range(4 * NY):
            target = (r + way(c % 2) * steps) % NZ
            pairs.append((r * 4 * NY + c, target * 4 * NY + c))
    return lax.ppermute(value, ("row", "col"), pairs)


def over_y(value, steps):
    pairs = []
    for c in range(4 * NY):
        pairs.append((c, ((c // 4 + way(c % 2) * steps) % NY) * 4 + c % 4))
    return lax.ppermute(value, "col", pairs)


def straight_y(value, steps):
    pairs = [(c, ((c // 4 + steps) % NY) * 4 + c % 4) for c in range(4 * NY)]
    return lax.ppermute(value, "col", pairs)


def col_swap(value, bit):
    return lax.ppermute(value, "col", [(c, c ^ bit) for c in range(4 * NY)])


def rep_swap(value):
    return lax.ppermute(value, "rep", [(0, 1), (1, 0)])


def over_x(value, steps):
    pairs = []
    for c in range(4 * NY):
        for p in range(2):
            x = (2 * p + (c // 2) % 2 + steps) % 4
            pairs.append((c * 2 + p, (c + 2 * (x % 2 - (c // 2) % 2)) * 2 + x // 2))
    return lax.ppermute(value, ("col", "rep"), pairs)


def spread(pattern_ref, rows, cols):
    pattern = pattern_ref[...].astype(F32).astype(BF16)
    rows_b, cols_b = pattern.shape
    left = (
        lax.broadcasted_iota(jnp.int32, (rows, rows_b), 0) // BLK
        == lax.broadcasted_iota(jnp.int32, (rows, rows_b), 1)
    )
    right = (
        lax.broadcasted_iota(jnp.int32, (cols_b, cols), 1) // BLK
        == lax.broadcasted_iota(jnp.int32, (cols_b, cols), 0)
    )
    wide = jnp.dot(pattern, right.astype(F32).astype(BF16), preferred_element_type=F32)
    return jnp.dot(
        left.astype(F32).astype(BF16), wide.astype(BF16), preferred_element_type=F32
    ).astype(BF16)


def mask_kernel(pattern_ref, matrix_ref, out_ref, *sums_refs):
    rows, cols = matrix_ref.shape
    masked = matrix_ref[...] * spread(pattern_ref, rows, cols)
    out_ref[...] = masked
    for ref in sums_refs:
        ref[...] = lax.dot_general(
            jnp.ones((8, cols), BF16), masked, (((1,), (1,)), ((), ())), preferred_element_type=F32
        )


def masked(name, pattern, matrix, with_sums=False):
    shapes = [jax.ShapeDtypeStruct(matrix.shape, BF16)]
    if with_sums:
        shapes.append(jax.ShapeDtypeStruct((8, matrix.shape[0]), F32))
    return pl.pallas_call(
        mask_kernel,
        out_shape=shapes,
        compiler_params=pltpu.CompilerParams(vmem_limit_bytes=12 * MIB),
        name=name,
    )(pattern, matrix)


def place():
    row = lax.axis_index("row")
    col = lax.axis_index("col")
    return row, col // 4, (col // 2) % 2, col % 2, lax.axis_index("rep")


def split_dot(wide, narrow):
    total = None
    for _ in range(3):
        piece = wide.astype(BF16)
        wide = wide - piece.astype(F32)
        term = lax.dot_general(
            piece, narrow, (((1,), (1,)), ((), ())), preferred_element_type=F32
        )
        total = term if total is None else total + term
    return total


def row_sums(ref):
    lanes = 128
    folded = ref[:, :lanes]
    for j in range(lanes, ref.shape[1], lanes):
        folded += ref[:, j : j + lanes]
    return lax.dot_general(
        jnp.ones((8, lanes), F32),
        folded,
        (((1,), (1,)), ((), ())),
        precision=lax.Precision.HIGHEST,
        preferred_element_type=F32,
    )


def early_kernel(*refs):
    n_ham, n_den = len(HAM_KEYS), len(DEN_KEYS) - 1
    ham_refs, den_refs, far_ref = refs[:n_ham], refs[n_ham : n_ham + n_den], refs[n_ham + n_den]
    other_ref, own_ref, ham_far_ref, sums_ref, den_buf = refs[n_ham + n_den + 1 :]
    row, y, x, core, rep = place()
    rows = own_ref.shape[0]
    for n in range(n_den):
        den_buf[lax.rem(row + way(core) * DEN_KEYS[n] + NZ, NZ)] = den_refs[n][...]
    far = lax.rem(row + NZ // 2, NZ)
    den_buf[far] = jnp.zeros(den_buf.shape[1:], BF16)
    half_size = den_buf.shape[1] // 2
    starts = [pl.multiple_of((1 - rep) * rows, rows), pl.multiple_of(rep * rows, rows)]
    for n, (dy, dx, dk) in enumerate(HAM_KEYS):
        half = core + dk - 2 * core * dk
        chip = lax.rem(y + way(half) * dy + NY, NY) * 2 + (x + dx - 2 * x * dx)
        block = ham_refs[n]

        @pl.when(chip == far)
        def _():
            ham_far_ref[half] = block[...]

        den = den_buf[chip, pl.ds(pl.multiple_of(half * half_size, half_size), half_size), :]
        for start, out_ref in zip(starts, (other_ref, own_ref)):
            term = jnp.dot(block[pl.ds(start, rows), :], den, preferred_element_type=F32)
            if n == 0:
                out_ref[...] = term
            else:
                out_ref[...] += term
    far_sums = split_dot(far_ref[:, :half_size], ham_far_ref[0])
    far_sums += split_dot(far_ref[:, half_size:], ham_far_ref[1])
    sums_ref[...] = far_sums
    for start, out_ref in zip(starts, (other_ref, own_ref)):
        sums_ref[:, pl.ds(start, rows)] += row_sums(out_ref)


def early(ham_blocks, den_blocks, far_sums):
    rows, half = ham_blocks[0].shape
    depth, cols = den_blocks[0].shape
    n = len(ham_blocks) + len(den_blocks) + 1
    return pl.pallas_call(
        early_kernel,
        out_shape=(
            jax.ShapeDtypeStruct((rows // 2, cols), F32),
            jax.ShapeDtypeStruct((rows // 2, cols), F32),
            jax.ShapeDtypeStruct((2, rows, half), BF16),
            jax.ShapeDtypeStruct((8, rows), F32),
        ),
        in_specs=[pl.BlockSpec(memory_space=pltpu.VMEM)] * n,
        scratch_shapes=[pltpu.VMEM((NZ, depth, cols), BF16)],
        compiler_params=pltpu.CompilerParams(vmem_limit_bytes=12 * MIB),
        cost_estimate=pl.CostEstimate(
            flops=2 * rows * cols * depth * NZ, bytes_accessed=4 * MIB, transcendentals=0
        ),
        name="early",
    )(*ham_blocks, *den_blocks, far_sums)


def late_kernel(other_ref, own_ref, ham_ref, den_ref, first_out, second_out, own_out):
    rep = lax.axis_index("rep")
    rows = own_out.shape[0]
    half = ham_ref.shape[2]
    cut = first_out.shape[0]
    for start, total in (((1 - rep) * rows, other_ref), (rep * rows, own_ref)):
        span = pl.ds(pl.multiple_of(start, rows), rows)
        term = jnp.dot(ham_ref[0, span], den_ref[:half], preferred_element_type=F32)
        term += jnp.dot(ham_ref[1, span], den_ref[half:], preferred_element_type=F32)
        if total is other_ref:
            first_out[...] = total[:cut] + term[:cut]
            second_out[...] = total[cut:] + term[cut:]
        else:
            own_out[...] = total[...] + term


def late(other, own, ham_far, den_far):
    rows, cols = own.shape
    return pl.pallas_call(
        late_kernel,
        out_shape=[jax.ShapeDtypeStruct((n, cols), F32) for n in (FIRST, rows - FIRST, rows)],
        in_specs=[pl.BlockSpec(memory_space=pltpu.VMEM)] * 4,
        compiler_params=pltpu.CompilerParams(vmem_limit_bytes=8 * MIB),
        name="late",
    )(other, own, ham_far, den_far)


def finish_kernel(kept_ref, first_ref, second_ref, out_ref):
    cut = first_ref.shape[0]
    out_ref[:cut] = (kept_ref[:cut] + first_ref[...]).astype(BF16)
    out_ref[cut:] = (kept_ref[cut:] + second_ref[...]).astype(BF16)


def finish(kept, first, second):
    return pl.pallas_call(
        finish_kernel,
        out_shape=jax.ShapeDtypeStruct(kept.shape, BF16),
        compiler_params=pltpu.CompilerParams(vmem_limit_bytes=8 * MIB),
        name="finish",
    )(kept, first, second)


HAM_KEYS = [(dy, dx, dk) for dx in range(2) for dy in (0, -1, 1, 2) for dk in range(2)]
DEN_KEYS = [0, -1, 1, -2, 2, -3, 3, -4]


def after(value, *others):
    return lax.optimization_barrier((value, *others))[0]


def gather(dens, ham, dens_sums):
    den, got, swapped = {0: dens}, {(0, 0): ham}, {}

    def swap(key, *others):
        swapped[key] = col_swap(after(got[key], *others), 1)

    den[-1], den[1] = over_row(dens, 1), over_row(dens, -1)
    got[(-1, 0)], got[(1, 0)] = over_y(ham, 1), over_y(ham, -1)
    got[(0, 1)] = col_swap(ham, 2)

    den[-2], den[2] = over_row(den[-1], 1), over_row(den[1], -1)
    got[(-1, 1)] = over_y(after(got[(0, 1)], got[(-1, 0)]), 1)
    got[(1, 1)] = over_y(after(got[(0, 1)], got[(1, 0)]), -1)
    far_sums = over_row(dens_sums, 4)
    swap((0, 0), den[-1])
    swap((0, 1), swapped[(0, 0)])

    den[-3], den[3] = over_row(den[-2], 1), over_row(den[2], -1)
    got[(2, 1)] = over_y(got[(-1, 1)], 1)
    got[(2, 0)] = over_y(after(got[(1, 0)], got[(1, 1)]), -1)
    swap((-1, 0), den[-2], swapped[(0, 1)], far_sums)
    swap((1, 0), swapped[(-1, 0)])

    den[-4] = over_row(den[-3], 1)
    swap((-1, 1), den[-3])
    swap((1, 1), swapped[(-1, 1)])
    swap((2, 0), den[3])
    swap((2, 1), swapped[(2, 0)])
    ham_blocks = [(swapped if dk else got)[(dy, dx)] for dy, dx, dk in HAM_KEYS]
    return [den[key] for key in DEN_KEYS], ham_blocks, far_sums


def shards(hamiltonian, density, ham_pattern, den_pattern, tile_basis, offsets):
    dens, dens_sums = masked("mask_dens", den_pattern, density, with_sums=True)
    (ham,) = masked("mask_ham", ham_pattern, hamiltonian)
    (*den_blocks, den_far), ham_blocks, far_sums = gather(dens, ham, dens_sums)
    other, own, ham_far, sums = early(ham_blocks, den_blocks, far_sums)

    sums = sums + over_x(sums, 1) + over_x(sums, -1) + over_x(sums, 2)
    first, second, kept = late(other, own, ham_far, den_far)
    first = rep_swap(first)
    second = rep_swap(after(second, sums))
    product = finish(kept, first, second)
    sums = sums + straight_y(sums, 1) + straight_y(sums, -1) + straight_y(sums, 2)
    sums = after(sums + col_swap(sums, 1), first)

    total_order = density.shape[1] * lax.axis_size("col")
    atoms = offsets.shape[0]
    amplitudes = (sums[0] * (1.0 / math.sqrt(total_order))).reshape(2 * atoms, -1)
    tiles = jnp.einsum(
        "am,mtp->atp", amplitudes, tile_basis.astype(F32), precision=lax.Precision.HIGHEST
    )
    rep = lax.axis_index("rep")
    theirs = rep_swap(offsets)
    both = jnp.where(rep == 0, jnp.stack([offsets, theirs]), jnp.stack([theirs, offsets]))
    planes = both[:, :, None] + jnp.arange(TX, dtype=jnp.int32)[None, None, :]
    onehot = (planes[..., None] == jnp.arange(SX + TX, dtype=jnp.int32)).astype(F32)
    extended = jnp.einsum(
        "satx,satp->sxp",
        onehot,
        tiles.reshape(2, atoms, *tiles.shape[1:]),
        precision=lax.Precision.HIGHEST,
    )
    across = lax.ppermute(extended[1, SX:], "row", [(i, (i + 1) % NZ) for i in range(NZ)])
    incoming = jnp.where(rep == 0, across, extended[0, SX:])
    own_planes = jnp.where(rep == 0, extended[0, :SX], extended[1, :SX])
    grid_density = jnp.concatenate([own_planes[:TX] + incoming, own_planes[TX:]], axis=0)

    return (product, grid_density)


def solution(mesh):
    in_specs = (
        P("row", ("rep", "col")),
        P(("rep", "row"), "col"),
        P("row", ("rep", "col")),
        P(("rep", "row"), "col"),
        P(None, None, "col"),
        P(("row", "rep")),
    )
    out_specs = (P(("row", "rep"), "col"), P(("row", "rep"), "col"))
    return jax.shard_map(shards, mesh=mesh, in_specs=in_specs, out_specs=out_specs, check_vma=False)
```

```python
import functools
import math

import jax
import jax.numpy as jnp
from jax import lax
from jax.experimental import pallas as pl
from jax.experimental.pallas import tpu as pltpu
from jax.sharding import PartitionSpec as P

SX = 32
TX = 16
BLK = 64
MIB = 1 << 20

NZ = 8
NY = 4
F32 = jnp.float32
BF16 = jnp.bfloat16
FIRST = 256


def way(core):
    return 1 - 2 * core


def over_row(value, steps):
    pairs = []
    for r in range(NZ):
        for c in range(4 * NY):
            target = (r + way(c % 2) * steps) % NZ
            pairs.append((r * 4 * NY + c, target * 4 * NY + c))
    return lax.ppermute(value, ("row", "col"), pairs)


def over_y(value, steps):
    pairs = []
    for c in range(4 * NY):
        pairs.append((c, ((c // 4 + way(c % 2) * steps) % NY) * 4 + c % 4))
    return lax.ppermute(value, "col", pairs)


def straight_y(value, steps):
    pairs = [(c, ((c // 4 + steps) % NY) * 4 + c % 4) for c in range(4 * NY)]
    return lax.ppermute(value, "col", pairs)


def col_swap(value, bit):
    return lax.ppermute(value, "col", [(c, c ^ bit) for c in range(4 * NY)])


def rep_swap(value):
    return lax.ppermute(value, "rep", [(0, 1), (1, 0)])


def over_x(value, steps):
    pairs = []
    for c in range(4 * NY):
        for p in range(2):
            x = (2 * p + (c // 2) % 2 + steps) % 4
            pairs.append((c * 2 + p, (c + 2 * (x % 2 - (c // 2) % 2)) * 2 + x // 2))
    return lax.ppermute(value, ("col", "rep"), pairs)


def spread(pattern_ref, rows, cols):
    pattern = pattern_ref[...].astype(F32).astype(BF16)
    rows_b, cols_b = pattern.shape
    left = (
        lax.broadcasted_iota(jnp.int32, (rows, rows_b), 0) // BLK
        == lax.broadcasted_iota(jnp.int32, (rows, rows_b), 1)
    )
    right = (
        lax.broadcasted_iota(jnp.int32, (cols_b, cols), 1) // BLK
        == lax.broadcasted_iota(jnp.int32, (cols_b, cols), 0)
    )
    wide = jnp.dot(pattern, right.astype(F32).astype(BF16), preferred_element_type=F32)
    return jnp.dot(
        left.astype(F32).astype(BF16), wide.astype(BF16), preferred_element_type=F32
    ).astype(BF16)


def mask_kernel(pattern_ref, matrix_ref, out_ref, *sums_refs):
    rows, cols = matrix_ref.shape
    masked = matrix_ref[...] * spread(pattern_ref, rows, cols)
    out_ref[...] = masked
    for ref in sums_refs:
        ref[...] = lax.dot_general(
            jnp.ones((8, cols), BF16), masked, (((1,), (1,)), ((), ())), preferred_element_type=F32
        )


def masked(name, pattern, matrix, with_sums=False):
    shapes = [jax.ShapeDtypeStruct(matrix.shape, BF16)]
    if with_sums:
        shapes.append(jax.ShapeDtypeStruct((8, matrix.shape[0]), F32))
    return pl.pallas_call(
        mask_kernel,
        out_shape=shapes,
        compiler_params=pltpu.CompilerParams(vmem_limit_bytes=12 * MIB),
        name=name,
    )(pattern, matrix)


def place():
    row = lax.axis_index("row")
    col = lax.axis_index("col")
    return row, col // 4, (col // 2) % 2, col % 2, lax.axis_index("rep")


def dot_transposed(left, right):
    return lax.dot_general(left, right, (((1,), (1,)), ((), ())), preferred_element_type=F32)


def split_dot(wide, narrow):
    rows = wide.shape[0]
    terms = []
    for _ in range(3):
        terms.append(wide.astype(BF16))
        wide = wide - terms[-1].astype(F32)
    result = dot_transposed(jnp.concatenate(terms, axis=0), narrow)
    return result[:rows] + (result[rows : 2 * rows] + result[2 * rows :])


def row_sums(ref):
    lanes = 128
    folded = ref[:, :lanes]
    for j in range(lanes, ref.shape[1], lanes):
        folded += ref[:, j : j + lanes]
    return lax.dot_general(
        jnp.ones((8, lanes), F32),
        folded,
        (((1,), (1,)), ((), ())),
        precision=lax.Precision.HIGHEST,
        preferred_element_type=F32,
    )


def early_kernel(*refs):
    n_ham, n_den = len(HAM_KEYS), len(DEN_KEYS) - 1
    ham_refs, den_refs, far_ref = refs[:n_ham], refs[n_ham : n_ham + n_den], refs[n_ham + n_den]
    other_out, own_out, ham_far_out, sums_ref, other_ref, own_ref, ham_far_ref, den_buf, sems = refs[
        n_ham + n_den + 1 :
    ]
    row, y, x, core, rep = place()
    rows = own_ref.shape[0]
    for n in range(n_den):
        den_buf[lax.rem(row + way(core) * DEN_KEYS[n] + NZ, NZ)] = den_refs[n][...]
    far = lax.rem(row + NZ // 2, NZ)
    den_buf[far] = jnp.zeros(den_buf.shape[1:], BF16)
    half_size = den_buf.shape[1] // 2
    places = []
    for n, (dy, dx, dk) in enumerate(HAM_KEYS):
        half = core + dk - 2 * core * dk
        chip = lax.rem(y + way(half) * dy + NY, NY) * 2 + (x + dx - 2 * x * dx)
        places.append((chip, half))

        @pl.when(chip == far)
        def _():
            ham_far_ref[half] = ham_refs[n][...]

    out = pltpu.make_async_copy(ham_far_ref, ham_far_out, sems.at[0])
    out.start()
    outs = [out]
    sums_ref[...] = split_dot(far_ref[:, :half_size], ham_far_ref[0]) + split_dot(
        far_ref[:, half_size:], ham_far_ref[1]
    )
    for i, (part, total, total_out) in enumerate(((1 - rep, other_ref, other_out), (rep, own_ref, own_out))):
        span = pl.ds(pl.multiple_of(part * rows, rows), rows)
        for n, (chip, half) in enumerate(places):
            den = den_buf[chip, pl.ds(pl.multiple_of(half * half_size, half_size), half_size), :]
            term = jnp.dot(ham_refs[n][span, :], den, preferred_element_type=F32)
            if n == 0:
                total[...] = term
            else:
                total[...] += term
        out = pltpu.make_async_copy(total, total_out, sems.at[1 + i])
        out.start()
        outs.append(out)
        sums_ref[:, span] += row_sums(total)
    for out in outs:
        out.wait()


def early(ham_blocks, den_blocks, far_sums):
    rows, half = ham_blocks[0].shape
    depth, cols = den_blocks[0].shape
    n = len(ham_blocks) + len(den_blocks) + 1
    shapes = [((rows // 2, cols), F32), ((rows // 2, cols), F32), ((2, rows, half), BF16)]
    return pl.pallas_call(
        early_kernel,
        out_shape=[jax.ShapeDtypeStruct(*shape) for shape in shapes] + [jax.ShapeDtypeStruct((8, rows), F32)],
        in_specs=[pl.BlockSpec(memory_space=pltpu.VMEM)] * n,
        out_specs=[pl.BlockSpec(memory_space=pltpu.HBM)] * 3 + [pl.BlockSpec(memory_space=pltpu.VMEM)],
        scratch_shapes=[pltpu.VMEM(*shape) for shape in shapes]
        + [pltpu.VMEM((NZ, depth, cols), BF16), pltpu.SemaphoreType.DMA((3,))],
        compiler_params=pltpu.CompilerParams(vmem_limit_bytes=16 * MIB),
        cost_estimate=pl.CostEstimate(
            flops=2 * rows * cols * depth * NZ, bytes_accessed=4 * MIB, transcendentals=0
        ),
        name="early",
    )(*ham_blocks, *den_blocks, far_sums)


def far_term(start, rows, ham_ref, den_ref):
    half = ham_ref.shape[2]
    span = pl.ds(pl.multiple_of(start, rows), rows)
    term = jnp.dot(ham_ref[0, span], den_ref[:half], preferred_element_type=F32)
    return term + jnp.dot(ham_ref[1, span], den_ref[half:], preferred_element_type=F32)


def late_kernel(other_ref, ham_ref, den_ref, first_out, second_out):
    rows, cut = other_ref.shape[0], first_out.shape[0]
    term = far_term((1 - lax.axis_index("rep")) * rows, rows, ham_ref, den_ref)
    first_out[...] = other_ref[:cut] + term[:cut]
    second_out[...] = other_ref[cut:] + term[cut:]


def late(other, ham_far, den_far):
    rows, cols = other.shape
    return pl.pallas_call(
        late_kernel,
        out_shape=[jax.ShapeDtypeStruct((n, cols), F32) for n in (FIRST, rows - FIRST)],
        in_specs=[pl.BlockSpec(memory_space=pltpu.VMEM)] * 3,
        compiler_params=pltpu.CompilerParams(vmem_limit_bytes=8 * MIB),
        name="late",
    )(other, ham_far, den_far)


def kept_kernel(own_ref, ham_ref, den_ref, out_ref):
    rows = own_ref.shape[0]
    out_ref[...] = own_ref[...] + far_term(lax.axis_index("rep") * rows, rows, ham_ref, den_ref)


def kept_rows(own, ham_far, den_far):
    return pl.pallas_call(
        kept_kernel,
        out_shape=jax.ShapeDtypeStruct(own.shape, F32),
        in_specs=[pl.BlockSpec(memory_space=pltpu.VMEM)] * 3,
        compiler_params=pltpu.CompilerParams(vmem_limit_bytes=8 * MIB),
        name="kept",
    )(own, ham_far, den_far)


def finish_kernel(kept_ref, first_ref, second_ref, out_ref):
    cut = first_ref.shape[0]
    out_ref[:cut] = (kept_ref[:cut] + first_ref[...]).astype(BF16)
    out_ref[cut:] = (kept_ref[cut:] + second_ref[...]).astype(BF16)


def finish(kept, first, second):
    return pl.pallas_call(
        finish_kernel,
        out_shape=jax.ShapeDtypeStruct(kept.shape, BF16),
        compiler_params=pltpu.CompilerParams(vmem_limit_bytes=8 * MIB),
        name="finish",
    )(kept, first, second)


HAM_KEYS = [(dy, dx, dk) for dx in range(2) for dy in (0, -1, 1, 2) for dk in range(2)]
DEN_KEYS = [0, -1, 1, -2, 2, -3, 3, -4]


def after(value, *others):
    return lax.optimization_barrier((value, *others))[0]


def gather(dens, ham, dens_sums):
    den, got, swapped = {0: dens}, {(0, 0): ham}, {}

    def swap(key, *others):
        swapped[key] = col_swap(after(got[key], *others), 1)

    den[-1], den[1] = over_row(dens, 1), over_row(dens, -1)
    got[(-1, 0)], got[(1, 0)] = over_y(ham, 1), over_y(ham, -1)
    got[(0, 1)] = col_swap(ham, 2)

    den[-2], den[2] = over_row(den[-1], 1), over_row(den[1], -1)
    got[(-1, 1)] = over_y(after(got[(0, 1)], got[(-1, 0)]), 1)
    got[(1, 1)] = over_y(after(got[(0, 1)], got[(1, 0)]), -1)
    far_sums = over_row(dens_sums, 4)
    swap((0, 0), den[-1])
    swap((0, 1), swapped[(0, 0)])

    den[-3], den[3] = over_row(den[-2], 1), over_row(den[2], -1)
    got[(2, 1)] = over_y(got[(-1, 1)], 1)
    got[(2, 0)] = over_y(after(got[(1, 0)], got[(1, 1)]), -1)
    swap((-1, 0), den[-2], swapped[(0, 1)], far_sums)
    swap((1, 0), swapped[(-1, 0)])

    den[-4] = over_row(den[-3], 1)
    swap((-1, 1), den[-3])
    swap((1, 1), swapped[(-1, 1)])
    swap((2, 0), den[3])
    swap((2, 1), swapped[(2, 0)])
    ham_blocks = [(swapped if dk else got)[(dy, dx)] for dy, dx, dk in HAM_KEYS]
    return [den[key] for key in DEN_KEYS], ham_blocks, far_sums


def shards(hamiltonian, density, ham_pattern, den_pattern, tile_basis, offsets):
    dens, dens_sums = masked("mask_dens", den_pattern, density, with_sums=True)
    (ham,) = masked("mask_ham", ham_pattern, hamiltonian)
    (*den_blocks, den_far), ham_blocks, far_sums = gather(dens, ham, dens_sums)
    other, own, ham_far, sums = early(ham_blocks, den_blocks, far_sums)

    atoms = offsets.shape[0]
    sums = sums.at[1, :atoms].set(offsets.astype(F32))
    hops = [over_x(sums, steps) for steps in (1, -1, 2)]
    theirs = hops[2][1, :atoms].astype(jnp.int32)
    sums = sums + hops[0] + hops[1] + hops[2]
    first, second = late(other, ham_far, den_far)
    first = rep_swap(first)
    second = rep_swap(after(second, sums))
    product = finish(kept_rows(after(own, first), ham_far, den_far), first, second)
    sums = sums + straight_y(sums, 1) + straight_y(sums, -1) + straight_y(sums, 2)
    sums = after(sums + col_swap(sums, 1), first)

    total_order = density.shape[1] * lax.axis_size("col")
    amplitudes = (sums[0] * (1.0 / math.sqrt(total_order))).reshape(2 * atoms, -1)
    tiles = jnp.einsum(
        "am,mtp->atp", amplitudes, tile_basis.astype(F32), precision=lax.Precision.HIGHEST
    )
    rep = lax.axis_index("rep")
    both = jnp.where(rep == 0, jnp.stack([offsets, theirs]), jnp.stack([theirs, offsets]))
    planes = both[:, :, None] + jnp.arange(TX, dtype=jnp.int32)[None, None, :]
    onehot = (planes[..., None] == jnp.arange(SX + TX, dtype=jnp.int32)).astype(F32)
    extended = jnp.einsum(
        "satx,satp->sxp",
        onehot,
        tiles.reshape(2, atoms, *tiles.shape[1:]),
        precision=lax.Precision.HIGHEST,
    )
    across = lax.ppermute(extended[1, SX:], "row", [(i, (i + 1) % NZ) for i in range(NZ)])
    incoming = jnp.where(rep == 0, across, extended[0, SX:])
    own_planes = jnp.where(rep == 0, extended[0, :SX], extended[1, :SX])
    grid_density = jnp.concatenate([own_planes[:TX] + incoming, own_planes[TX:]], axis=0)

    return (product, grid_density)


def solution(mesh):
    in_specs = (
        P("row", ("rep", "col")),
        P(("rep", "row"), "col"),
        P("row", ("rep", "col")),
        P(("rep", "row"), "col"),
        P(None, None, "col"),
        P(("row", "rep")),
    )
    out_specs = (P(("row", "rep"), "col"), P(("row", "rep"), "col"))
    return jax.shard_map(shards, mesh=mesh, in_specs=in_specs, out_specs=out_specs, check_vma=False)
```

```python
import functools
import math

import jax
import jax.numpy as jnp
from jax import lax
from jax.experimental import pallas as pl
from jax.experimental.pallas import tpu as pltpu
from jax.sharding import PartitionSpec as P

SX = 32
TX = 16
BLK = 64
MIB = 1 << 20

NZ = 8
NY = 4
F32 = jnp.float32
BF16 = jnp.bfloat16
FIRST = 256


def way(core):
    return 1 - 2 * core


def over_row(value, steps):
    pairs = []
    for r in range(NZ):
        for c in range(4 * NY):
            target = (r + way(c % 2) * steps) % NZ
            pairs.append((r * 4 * NY + c, target * 4 * NY + c))
    return lax.ppermute(value, ("row", "col"), pairs)


def over_y(value, steps):
    pairs = []
    for c in range(4 * NY):
        pairs.append((c, ((c // 4 + way(c % 2) * steps) % NY) * 4 + c % 4))
    return lax.ppermute(value, "col", pairs)


def straight_y(value, steps):
    pairs = [(c, ((c // 4 + steps) % NY) * 4 + c % 4) for c in range(4 * NY)]
    return lax.ppermute(value, "col", pairs)


def col_swap(value, bit):
    return lax.ppermute(value, "col", [(c, c ^ bit) for c in range(4 * NY)])


def rep_swap(value):
    return lax.ppermute(value, "rep", [(0, 1), (1, 0)])


def over_x(value, steps):
    pairs = []
    for c in range(4 * NY):
        for p in range(2):
            x = (2 * p + (c // 2) % 2 + steps) % 4
            pairs.append((c * 2 + p, (c + 2 * (x % 2 - (c // 2) % 2)) * 2 + x // 2))
    return lax.ppermute(value, ("col", "rep"), pairs)


def spread(pattern_ref, rows, cols):
    pattern = pattern_ref[...].astype(F32).astype(BF16)
    rows_b, cols_b = pattern.shape
    left = (
        lax.broadcasted_iota(jnp.int32, (rows, rows_b), 0) // BLK
        == lax.broadcasted_iota(jnp.int32, (rows, rows_b), 1)
    )
    right = (
        lax.broadcasted_iota(jnp.int32, (cols_b, cols), 1) // BLK
        == lax.broadcasted_iota(jnp.int32, (cols_b, cols), 0)
    )
    wide = jnp.dot(pattern, right.astype(F32).astype(BF16), preferred_element_type=F32)
    return jnp.dot(
        left.astype(F32).astype(BF16), wide.astype(BF16), preferred_element_type=F32
    ).astype(BF16)


def mask_kernel(pattern_ref, matrix_ref, out_ref, *sums_refs):
    rows, cols = matrix_ref.shape
    masked = matrix_ref[...] * spread(pattern_ref, rows, cols)
    out_ref[...] = masked
    for ref in sums_refs:
        ref[...] = lax.dot_general(
            jnp.ones((8, cols), BF16), masked, (((1,), (1,)), ((), ())), preferred_element_type=F32
        )


def masked(name, pattern, matrix, with_sums=False):
    shapes = [jax.ShapeDtypeStruct(matrix.shape, BF16)]
    if with_sums:
        shapes.append(jax.ShapeDtypeStruct((8, matrix.shape[0]), F32))
    return pl.pallas_call(
        mask_kernel,
        out_shape=shapes,
        compiler_params=pltpu.CompilerParams(vmem_limit_bytes=12 * MIB),
        name=name,
    )(pattern, matrix)


def place():
    row = lax.axis_index("row")
    col = lax.axis_index("col")
    return row, col // 4, (col // 2) % 2, col % 2, lax.axis_index("rep")


def dot_transposed(left, right):
    return lax.dot_general(left, right, (((1,), (1,)), ((), ())), preferred_element_type=F32)


def split_dot(wide, narrow):
    rows = wide.shape[0]
    terms = []
    for _ in range(3):
        terms.append(wide.astype(BF16))
        wide = wide - terms[-1].astype(F32)
    result = dot_transposed(jnp.concatenate(terms, axis=0), narrow)
    return result[:rows] + (result[rows : 2 * rows] + result[2 * rows :])


def row_sums(ref):
    lanes = 128
    folded = ref[:, :lanes]
    for j in range(lanes, ref.shape[1], lanes):
        folded += ref[:, j : j + lanes]
    return lax.dot_general(
        jnp.ones((8, lanes), F32),
        folded,
        (((1,), (1,)), ((), ())),
        precision=lax.Precision.HIGHEST,
        preferred_element_type=F32,
    )


def early_kernel(*refs):
    n_ham, n_den = len(HAM_KEYS), len(DEN_KEYS) - 1
    ham_refs, den_refs, far_ref = refs[:n_ham], refs[n_ham : n_ham + n_den], refs[n_ham + n_den]
    other_out, own_ref, ham_far_ref, sums_ref, other_ref, den_buf, sem = refs[n_ham + n_den + 1 :]
    row, y, x, core, rep = place()
    rows = own_ref.shape[0]
    for n in range(n_den):
        den_buf[lax.rem(row + way(core) * DEN_KEYS[n] + NZ, NZ)] = den_refs[n][...]
    far = lax.rem(row + NZ // 2, NZ)
    den_buf[far] = jnp.zeros(den_buf.shape[1:], BF16)
    half_size = den_buf.shape[1] // 2
    places = []
    for n, (dy, dx, dk) in enumerate(HAM_KEYS):
        half = core + dk - 2 * core * dk
        chip = lax.rem(y + way(half) * dy + NY, NY) * 2 + (x + dx - 2 * x * dx)
        places.append((chip, half))

        @pl.when(chip == far)
        def _():
            ham_far_ref[half] = ham_refs[n][...]

    sums_ref[...] = split_dot(far_ref[:, :half_size], ham_far_ref[0]) + split_dot(
        far_ref[:, half_size:], ham_far_ref[1]
    )
    out = pltpu.make_async_copy(other_ref, other_out, sem)
    for part, total in ((1 - rep, other_ref), (rep, own_ref)):
        span = pl.ds(pl.multiple_of(part * rows, rows), rows)
        for n, (chip, half) in enumerate(places):
            den = den_buf[chip, pl.ds(pl.multiple_of(half * half_size, half_size), half_size), :]
            term = jnp.dot(ham_refs[n][span, :], den, preferred_element_type=F32)
            if n == 0:
                total[...] = term
            else:
                total[...] += term
        if total is other_ref:
            out.start()
        sums_ref[:, span] += row_sums(total)
    out.wait()


def early(ham_blocks, den_blocks, far_sums):
    rows, half = ham_blocks[0].shape
    depth, cols = den_blocks[0].shape
    n = len(ham_blocks) + len(den_blocks) + 1
    shapes = [((rows // 2, cols), F32), ((rows // 2, cols), F32), ((2, rows, half), BF16)]
    return pl.pallas_call(
        early_kernel,
        out_shape=[pltpu.HBM(*shapes[0])]
        + [jax.ShapeDtypeStruct(*shape) for shape in shapes[1:]]
        + [jax.ShapeDtypeStruct((8, rows), F32)],
        in_specs=[pl.BlockSpec(memory_space=pltpu.VMEM)] * n,
        out_specs=[pl.BlockSpec(memory_space=pltpu.HBM)] + [pl.BlockSpec(memory_space=pltpu.VMEM)] * 3,
        scratch_shapes=[
            pltpu.VMEM(*shapes[0]),
            pltpu.VMEM((NZ, depth, cols), BF16),
            pltpu.SemaphoreType.DMA,
        ],
        compiler_params=pltpu.CompilerParams(vmem_limit_bytes=16 * MIB),
        cost_estimate=pl.CostEstimate(
            flops=2 * rows * cols * depth * NZ, bytes_accessed=4 * MIB, transcendentals=0
        ),
        name="early",
    )(*ham_blocks, *den_blocks, far_sums)


def far_term(start, rows, ham_ref, den_ref):
    half = ham_ref.shape[2]
    span = pl.ds(pl.multiple_of(start, rows), rows)
    term = jnp.dot(ham_ref[0, span], den_ref[:half], preferred_element_type=F32)
    return term + jnp.dot(ham_ref[1, span], den_ref[half:], preferred_element_type=F32)


def late_kernel(other_ref, ham_ref, den_ref, first_out, second_out, other_buf, sem):
    rows, cut = other_ref.shape[0], first_out.shape[0]
    copy = pltpu.make_async_copy(other_ref, other_buf, sem)
    copy.start()
    term = far_term((1 - lax.axis_index("rep")) * rows, rows, ham_ref, den_ref)
    copy.wait()
    first_out[...] = other_buf[:cut] + term[:cut]
    second_out[...] = other_buf[cut:] + term[cut:]


def late(other, ham_far, den_far):
    rows, cols = other.shape
    return pl.pallas_call(
        late_kernel,
        out_shape=[jax.ShapeDtypeStruct((n, cols), F32) for n in (FIRST, rows - FIRST)],
        in_specs=[pl.BlockSpec(memory_space=pltpu.HBM)] + [pl.BlockSpec(memory_space=pltpu.VMEM)] * 2,
        scratch_shapes=[pltpu.VMEM((rows, cols), F32), pltpu.SemaphoreType.DMA],
        compiler_params=pltpu.CompilerParams(vmem_limit_bytes=8 * MIB),
        name="late",
    )(pltpu.with_memory_space_constraint(other, pltpu.HBM), ham_far, den_far)


def kept_kernel(own_ref, ham_ref, den_ref, out_ref):
    rows = own_ref.shape[0]
    out_ref[...] = own_ref[...] + far_term(lax.axis_index("rep") * rows, rows, ham_ref, den_ref)


def kept_rows(own, ham_far, den_far):
    return pl.pallas_call(
        kept_kernel,
        out_shape=jax.ShapeDtypeStruct(own.shape, F32),
        in_specs=[pl.BlockSpec(memory_space=pltpu.VMEM)] * 3,
        compiler_params=pltpu.CompilerParams(vmem_limit_bytes=8 * MIB),
        name="kept",
    )(own, ham_far, den_far)


def finish_kernel(kept_ref, first_ref, second_ref, out_ref):
    cut = first_ref.shape[0]
    out_ref[:cut] = (kept_ref[:cut] + first_ref[...]).astype(BF16)
    out_ref[cut:] = (kept_ref[cut:] + second_ref[...]).astype(BF16)


def finish(kept, first, second):
    return pl.pallas_call(
        finish_kernel,
        out_shape=jax.ShapeDtypeStruct(kept.shape, BF16),
        compiler_params=pltpu.CompilerParams(vmem_limit_bytes=8 * MIB),
        name="finish",
    )(kept, first, second)


HAM_KEYS = [(dy, dx, dk) for dx in range(2) for dy in (0, -1, 1, 2) for dk in range(2)]
DEN_KEYS = [0, -1, 1, -2, 2, -3, 3, -4]


def after(value, *others):
    return lax.optimization_barrier((value, *others))[0]


def gather(dens, ham, dens_sums):
    den, got, swapped = {0: dens}, {(0, 0): ham}, {}

    def swap(key, *others):
        swapped[key] = col_swap(after(got[key], *others), 1)

    den[-1], den[1] = over_row(dens, 1), over_row(dens, -1)
    got[(-1, 0)], got[(1, 0)] = over_y(ham, 1), over_y(ham, -1)
    got[(0, 1)] = col_swap(ham, 2)

    den[-2], den[2] = over_row(den[-1], 1), over_row(den[1], -1)
    got[(-1, 1)] = over_y(after(got[(0, 1)], got[(-1, 0)]), 1)
    got[(1, 1)] = over_y(after(got[(0, 1)], got[(1, 0)]), -1)
    far_sums = over_row(dens_sums, 4)
    swap((0, 0), den[-1])
    swap((0, 1), swapped[(0, 0)])

    den[-3], den[3] = over_row(den[-2], 1), over_row(den[2], -1)
    got[(2, 1)] = over_y(got[(-1, 1)], 1)
    got[(2, 0)] = over_y(after(got[(1, 0)], got[(1, 1)]), -1)
    swap((-1, 0), den[-2], swapped[(0, 1)], far_sums)
    swap((1, 0), swapped[(-1, 0)])

    den[-4] = over_row(den[-3], 1)
    swap((-1, 1), den[-3])
    swap((1, 1), swapped[(-1, 1)])
    swap((2, 0), den[3])
    swap((2, 1), swapped[(2, 0)])
    ham_blocks = [(swapped if dk else got)[(dy, dx)] for dy, dx, dk in HAM_KEYS]
    return [den[key] for key in DEN_KEYS], ham_blocks, far_sums


def shards(hamiltonian, density, ham_pattern, den_pattern, tile_basis, offsets):
    dens, dens_sums = masked("mask_dens", den_pattern, density, with_sums=True)
    (ham,) = masked("mask_ham", ham_pattern, hamiltonian)
    (*den_blocks, den_far), ham_blocks, far_sums = gather(dens, ham, dens_sums)
    other, own, ham_far, sums = early(ham_blocks, den_blocks, far_sums)

    atoms = offsets.shape[0]
    sums = sums.at[1, :atoms].set(offsets.astype(F32))
    hops = [over_x(sums, steps) for steps in (1, -1, 2)]
    theirs = hops[2][1, :atoms].astype(jnp.int32)
    sums = sums + hops[0] + hops[1] + hops[2]
    first, second = late(other, ham_far, den_far)
    first = rep_swap(first)
    second = rep_swap(after(second, sums))
    product = finish(kept_rows(after(own, first), ham_far, den_far), first, second)
    sums = sums + straight_y(sums, 1) + straight_y(sums, -1) + straight_y(sums, 2)
    sums = after(sums + col_swap(sums, 1), first)

    total_order = density.shape[1] * lax.axis_size("col")
    amplitudes = (sums[0] * (1.0 / math.sqrt(total_order))).reshape(2 * atoms, -1)
    tiles = jnp.einsum(
        "am,mtp->atp", amplitudes, tile_basis.astype(F32), precision=lax.Precision.HIGHEST
    )
    rep = lax.axis_index("rep")
    both = jnp.where(rep == 0, jnp.stack([offsets, theirs]), jnp.stack([theirs, offsets]))
    planes = both[:, :, None] + jnp.arange(TX, dtype=jnp.int32)[None, None, :]
    onehot = (planes[..., None] == jnp.arange(SX + TX, dtype=jnp.int32)).astype(F32)
    extended = jnp.einsum(
        "satx,satp->sxp",
        onehot,
        tiles.reshape(2, atoms, *tiles.shape[1:]),
        precision=lax.Precision.HIGHEST,
    )
    across = lax.ppermute(extended[1, SX:], "row", [(i, (i + 1) % NZ) for i in range(NZ)])
    incoming = jnp.where(rep == 0, across, extended[0, SX:])
    own_planes = jnp.where(rep == 0, extended[0, :SX], extended[1, :SX])
    grid_density = jnp.concatenate([own_planes[:TX] + incoming, own_planes[TX:]], axis=0)

    return (product, grid_density)


def solution(mesh):
    in_specs = (
        P("row", ("rep", "col")),
        P(("rep", "row"), "col"),
        P("row", ("rep", "col")),
        P(("rep", "row"), "col"),
        P(None, None, "col"),
        P(("row", "rep")),
    )
    out_specs = (P(("row", "rep"), "col"), P(("row", "rep"), "col"))
    return jax.shard_map(shards, mesh=mesh, in_specs=in_specs, out_specs=out_specs, check_vma=False)
```

```python
import functools
import math

import jax
import jax.numpy as jnp
from jax import lax
from jax.experimental import pallas as pl
from jax.experimental.pallas import tpu as pltpu
from jax.sharding import PartitionSpec as P

SX = 32
TX = 16
BLK = 64
MIB = 1 << 20

NZ = 8
NY = 4
F32 = jnp.float32
BF16 = jnp.bfloat16
FIRST = 288


def way(core):
    return 1 - 2 * core


def over_row(value, steps):
    pairs = []
    for r in range(NZ):
        for c in range(4 * NY):
            target = (r + way(c % 2) * steps) % NZ
            pairs.append((r * 4 * NY + c, target * 4 * NY + c))
    return lax.ppermute(value, ("row", "col"), pairs)


def over_y(value, steps):
    pairs = []
    for c in range(4 * NY):
        pairs.append((c, ((c // 4 + way(c % 2) * steps) % NY) * 4 + c % 4))
    return lax.ppermute(value, "col", pairs)


def straight_y(value, steps):
    pairs = [(c, ((c // 4 + steps) % NY) * 4 + c % 4) for c in range(4 * NY)]
    return lax.ppermute(value, "col", pairs)


def col_swap(value, bit):
    return lax.ppermute(value, "col", [(c, c ^ bit) for c in range(4 * NY)])


def rep_swap(value):
    return lax.ppermute(value, "rep", [(0, 1), (1, 0)])


def over_x(value, steps):
    pairs = []
    for c in range(4 * NY):
        for p in range(2):
            x = (2 * p + (c // 2) % 2 + steps) % 4
            pairs.append((c * 2 + p, (c + 2 * (x % 2 - (c // 2) % 2)) * 2 + x // 2))
    return lax.ppermute(value, ("col", "rep"), pairs)


def spread(pattern_ref, rows, cols):
    pattern = pattern_ref[...].astype(F32).astype(BF16)
    rows_b, cols_b = pattern.shape
    left = (
        lax.broadcasted_iota(jnp.int32, (rows, rows_b), 0) // BLK
        == lax.broadcasted_iota(jnp.int32, (rows, rows_b), 1)
    )
    right = (
        lax.broadcasted_iota(jnp.int32, (cols_b, cols), 1) // BLK
        == lax.broadcasted_iota(jnp.int32, (cols_b, cols), 0)
    )
    wide = jnp.dot(pattern, right.astype(F32).astype(BF16), preferred_element_type=F32)
    return jnp.dot(
        left.astype(F32).astype(BF16), wide.astype(BF16), preferred_element_type=F32
    ).astype(BF16)


def mask_kernel(pattern_ref, matrix_ref, out_ref, *sums_refs):
    rows, cols = matrix_ref.shape
    masked = matrix_ref[...] * spread(pattern_ref, rows, cols)
    out_ref[...] = masked
    for ref in sums_refs:
        ref[...] = lax.dot_general(
            jnp.ones((8, cols), BF16), masked, (((1,), (1,)), ((), ())), preferred_element_type=F32
        )


def masked(name, pattern, matrix, with_sums=False):
    shapes = [jax.ShapeDtypeStruct(matrix.shape, BF16)]
    if with_sums:
        shapes.append(jax.ShapeDtypeStruct((8, matrix.shape[0]), F32))
    return pl.pallas_call(
        mask_kernel,
        out_shape=shapes,
        compiler_params=pltpu.CompilerParams(vmem_limit_bytes=12 * MIB),
        name=name,
    )(pattern, matrix)


def place():
    row = lax.axis_index("row")
    col = lax.axis_index("col")
    return row, col // 4, (col // 2) % 2, col % 2, lax.axis_index("rep")


def dot_transposed(left, right):
    return lax.dot_general(left, right, (((1,), (1,)), ((), ())), preferred_element_type=F32)


def split_dot(wide, narrow):
    rows = wide.shape[0]
    terms = []
    for _ in range(3):
        terms.append(wide.astype(BF16))
        wide = wide - terms[-1].astype(F32)
    result = dot_transposed(jnp.concatenate(terms, axis=0), narrow)
    return result[:rows] + (result[rows : 2 * rows] + result[2 * rows :])


def row_sums(ref):
    lanes = 128
    folded = ref[:, :lanes]
    for j in range(lanes, ref.shape[1], lanes):
        folded += ref[:, j : j + lanes]
    return lax.dot_general(
        jnp.ones((8, lanes), F32),
        folded,
        (((1,), (1,)), ((), ())),
        precision=lax.Precision.HIGHEST,
        preferred_element_type=F32,
    )


def early_kernel(*refs):
    n_ham, n_den = len(HAM_KEYS), len(DEN_KEYS) - 1
    ham_refs, den_refs, far_ref = refs[:n_ham], refs[n_ham : n_ham + n_den], refs[n_ham + n_den]
    other_out, own_ref, ham_far_ref, sums_ref, other_ref, den_buf, sem = refs[n_ham + n_den + 1 :]
    row, y, x, core, rep = place()
    rows = own_ref.shape[0]
    for n in range(n_den):
        den_buf[lax.rem(row + way(core) * DEN_KEYS[n] + NZ, NZ)] = den_refs[n][...]
    far = lax.rem(row + NZ // 2, NZ)
    den_buf[far] = jnp.zeros(den_buf.shape[1:], BF16)
    half_size = den_buf.shape[1] // 2
    places = []
    for n, (dy, dx, dk) in enumerate(HAM_KEYS):
        half = core + dk - 2 * core * dk
        chip = lax.rem(y + way(half) * dy + NY, NY) * 2 + (x + dx - 2 * x * dx)
        places.append((chip, half))

        @pl.when(chip == far)
        def _():
            ham_far_ref[half] = ham_refs[n][...]

    sums_ref[...] = split_dot(far_ref[:, :half_size], ham_far_ref[0]) + split_dot(
        far_ref[:, half_size:], ham_far_ref[1]
    )
    out = pltpu.make_async_copy(other_ref, other_out, sem)
    for part, total in ((1 - rep, other_ref), (rep, own_ref)):
        span = pl.ds(pl.multiple_of(part * rows, rows), rows)
        for n, (chip, half) in enumerate(places):
            den = den_buf[chip, pl.ds(pl.multiple_of(half * half_size, half_size), half_size), :]
            term = jnp.dot(ham_refs[n][span, :], den, preferred_element_type=F32)
            if n == 0:
                total[...] = term
            else:
                total[...] += term
        if total is other_ref:
            out.start()
        sums_ref[:, span] += row_sums(total)
    out.wait()


def early(ham_blocks, den_blocks, far_sums):
    rows, half = ham_blocks[0].shape
    depth, cols = den_blocks[0].shape
    n = len(ham_blocks) + len(den_blocks) + 1
    shapes = [((rows // 2, cols), F32), ((rows // 2, cols), F32), ((2, rows, half), BF16)]
    return pl.pallas_call(
        early_kernel,
        out_shape=[pltpu.HBM(*shapes[0])]
        + [jax.ShapeDtypeStruct(*shape) for shape in shapes[1:]]
        + [jax.ShapeDtypeStruct((8, rows), F32)],
        in_specs=[pl.BlockSpec(memory_space=pltpu.VMEM)] * n,
        out_specs=[pl.BlockSpec(memory_space=pltpu.HBM)] + [pl.BlockSpec(memory_space=pltpu.VMEM)] * 3,
        scratch_shapes=[
            pltpu.VMEM(*shapes[0]),
            pltpu.VMEM((NZ, depth, cols), BF16),
            pltpu.SemaphoreType.DMA,
        ],
        compiler_params=pltpu.CompilerParams(vmem_limit_bytes=16 * MIB),
        cost_estimate=pl.CostEstimate(
            flops=2 * rows * cols * depth * NZ, bytes_accessed=4 * MIB, transcendentals=0
        ),
        name="early",
    )(*ham_blocks, *den_blocks, far_sums)


def far_term(start, rows, ham_ref, den_ref):
    half = ham_ref.shape[2]
    span = pl.ds(pl.multiple_of(start, rows), rows)
    term = jnp.dot(ham_ref[0, span], den_ref[:half], preferred_element_type=F32)
    return term + jnp.dot(ham_ref[1, span], den_ref[half:], preferred_element_type=F32)


def late_kernel(other_ref, ham_ref, den_ref, first_out, second_out, other_buf, sem):
    rows, cut = other_ref.shape[0], first_out.shape[0]
    copy = pltpu.make_async_copy(other_ref, other_buf, sem)
    copy.start()
    term = far_term((1 - lax.axis_index("rep")) * rows, rows, ham_ref, den_ref)
    copy.wait()
    first_out[...] = other_buf[:cut] + term[:cut]
    second_out[...] = other_buf[cut:] + term[cut:]


def late(other, ham_far, den_far):
    rows, cols = other.shape
    return pl.pallas_call(
        late_kernel,
        out_shape=[jax.ShapeDtypeStruct((n, cols), F32) for n in (FIRST, rows - FIRST)],
        in_specs=[pl.BlockSpec(memory_space=pltpu.HBM)] + [pl.BlockSpec(memory_space=pltpu.VMEM)] * 2,
        scratch_shapes=[pltpu.VMEM((rows, cols), F32), pltpu.SemaphoreType.DMA],
        compiler_params=pltpu.CompilerParams(vmem_limit_bytes=8 * MIB),
        name="late",
    )(pltpu.with_memory_space_constraint(other, pltpu.HBM), ham_far, den_far)


def kept_kernel(own_ref, ham_ref, den_ref, out_ref):
    rows = own_ref.shape[0]
    out_ref[...] = own_ref[...] + far_term(lax.axis_index("rep") * rows, rows, ham_ref, den_ref)


def kept_rows(own, ham_far, den_far):
    return pl.pallas_call(
        kept_kernel,
        out_shape=jax.ShapeDtypeStruct(own.shape, F32),
        in_specs=[pl.BlockSpec(memory_space=pltpu.VMEM)] * 3,
        compiler_params=pltpu.CompilerParams(vmem_limit_bytes=8 * MIB),
        name="kept",
    )(own, ham_far, den_far)


def finish_kernel(kept_ref, first_ref, second_ref, out_ref):
    cut = first_ref.shape[0]
    out_ref[:cut] = (kept_ref[:cut] + first_ref[...]).astype(BF16)
    out_ref[cut:] = (kept_ref[cut:] + second_ref[...]).astype(BF16)


def finish(kept, first, second):
    return pl.pallas_call(
        finish_kernel,
        out_shape=jax.ShapeDtypeStruct(kept.shape, BF16),
        compiler_params=pltpu.CompilerParams(vmem_limit_bytes=8 * MIB),
        name="finish",
    )(kept, first, second)


HAM_KEYS = [(dy, dx, dk) for dx in range(2) for dy in (0, -1, 1, 2) for dk in range(2)]
DEN_KEYS = [0, -1, 1, -2, 2, -3, 3, -4]


def after(value, *others):
    return lax.optimization_barrier((value, *others))[0]


def gather(dens, ham, dens_sums):
    den, got, swapped = {0: dens}, {(0, 0): ham}, {}

    def swap(key, *others):
        swapped[key] = col_swap(after(got[key], *others), 1)

    den[-1], den[1] = over_row(dens, 1), over_row(dens, -1)
    got[(-1, 0)], got[(1, 0)] = over_y(ham, 1), over_y(ham, -1)
    got[(0, 1)] = col_swap(ham, 2)

    den[-2], den[2] = over_row(den[-1], 1), over_row(den[1], -1)
    got[(-1, 1)] = over_y(after(got[(0, 1)], got[(-1, 0)]), 1)
    got[(1, 1)] = over_y(after(got[(0, 1)], got[(1, 0)]), -1)
    far_sums = over_row(dens_sums, 4)
    swap((0, 0), den[-1])
    swap((0, 1), swapped[(0, 0)])

    den[-3], den[3] = over_row(den[-2], 1), over_row(den[2], -1)
    got[(2, 1)] = over_y(got[(-1, 1)], 1)
    got[(2, 0)] = over_y(after(got[(1, 0)], got[(1, 1)]), -1)
    swap((-1, 0), den[-2], swapped[(0, 1)], far_sums)
    swap((1, 0), swapped[(-1, 0)])

    den[-4] = over_row(den[-3], 1)
    swap((-1, 1), den[-3])
    swap((1, 1), swapped[(-1, 1)])
    swap((2, 0), den[3])
    swap((2, 1), swapped[(2, 0)])
    ham_blocks = [(swapped if dk else got)[(dy, dx)] for dy, dx, dk in HAM_KEYS]
    return [den[key] for key in DEN_KEYS], ham_blocks, far_sums


def shards(hamiltonian, density, ham_pattern, den_pattern, tile_basis, offsets):
    dens, dens_sums = masked("mask_dens", den_pattern, density, with_sums=True)
    (ham,) = masked("mask_ham", ham_pattern, hamiltonian)
    (*den_blocks, den_far), ham_blocks, far_sums = gather(dens, ham, dens_sums)
    other, own, ham_far, sums = early(ham_blocks, den_blocks, far_sums)

    atoms = offsets.shape[0]
    sums = sums.at[1, :atoms].set(offsets.astype(F32))
    hops = [over_x(sums, steps) for steps in (1, -1, 2)]
    theirs = hops[2][1, :atoms].astype(jnp.int32)
    sums = sums + hops[0] + hops[1] + hops[2]
    first, second = late(other, ham_far, den_far)
    first = rep_swap(first)
    second = rep_swap(after(second, sums))
    product = finish(kept_rows(after(own, first), ham_far, den_far), first, second)
    sums = sums + straight_y(sums, 1) + straight_y(sums, -1) + straight_y(sums, 2)
    sums = after(sums + col_swap(sums, 1), first)

    total_order = density.shape[1] * lax.axis_size("col")
    amplitudes = (sums[0] * (1.0 / math.sqrt(total_order))).reshape(2 * atoms, -1)
    tiles = jnp.einsum(
        "am,mtp->atp", amplitudes, tile_basis.astype(F32), precision=lax.Precision.HIGHEST
    )
    rep = lax.axis_index("rep")
    both = jnp.where(rep == 0, jnp.stack([offsets, theirs]), jnp.stack([theirs, offsets]))
    planes = both[:, :, None] + jnp.arange(TX, dtype=jnp.int32)[None, None, :]
    onehot = (planes[..., None] == jnp.arange(SX + TX, dtype=jnp.int32)).astype(F32)
    extended = jnp.einsum(
        "satx,satp->sxp",
        onehot,
        tiles.reshape(2, atoms, *tiles.shape[1:]),
        precision=lax.Precision.HIGHEST,
    )
    across = lax.ppermute(extended[1, SX:], "row", [(i, (i + 1) % NZ) for i in range(NZ)])
    incoming = jnp.where(rep == 0, across, extended[0, SX:])
    own_planes = jnp.where(rep == 0, extended[0, :SX], extended[1, :SX])
    grid_density = jnp.concatenate([own_planes[:TX] + incoming, own_planes[TX:]], axis=0)

    return (product, grid_density)


def solution(mesh):
    in_specs = (
        P("row", ("rep", "col")),
        P(("rep", "row"), "col"),
        P("row", ("rep", "col")),
        P(("rep", "row"), "col"),
        P(None, None, "col"),
        P(("row", "rep")),
    )
    out_specs = (P(("row", "rep"), "col"), P(("row", "rep"), "col"))
    return jax.shard_map(shards, mesh=mesh, in_specs=in_specs, out_specs=out_specs, check_vma=False)
```
